512 devices in a mesh: dp: 64 (over z, y_lo, core), tensor: 8 (over y_hi, x).
Axes of the slice: x: 4, y: 4 (y_hi: 2, y_lo: 2; y = y_hi * 2 + y_lo), z: 16, core: 2. Of those that a mesh axis runs over, the one named last changes fastest.
Arguments:
- gradient: bfloat16 [512, 262144], P(None, ('dp', 'tensor')), may hold values from -110 to 110
- owner_table: int32 [512], replicated, may hold values from 0 to 511, as said below
- prev_stats: bfloat16 [1024, 2, 512, 512], P(('dp', 'tensor')), may hold values from -16 to 8192, as said below
Outputs:
- update: bfloat16 [512, 262144], P(None, ('dp', 'tensor'))
The draws below stay inside these ranges and needn't reach their ends.
Inputs may be any that keep to these rules, and one draw needn't show every extreme that they name: `owner_table`: a device index with dp major; a quarter of the devices own exactly 2 blocks each, a half own exactly half as many each, the remaining quarter own none. `prev_stats`: every matrix is symmetric and its diagonal entry exceeds the sum of the magnitudes of the other entries of its row; slots that no block takes are never read.
All inputs are finite; a program needn't handle non-finite values.
Results may differ from the reference program's by a relative error of at most 0.0014.
The reference program's roundings to bfloat16 on the way count: a program that leaves them out, or rounds other values in their place, can miss the bound.
Values may be sent and summed in bfloat16 or wider, within the bound.
A program may use at most 64 MiB of HBM per device.

```python
import math
import jax
import jax.numpy as jnp
from jax import lax

BLK = 512
ITERS = 2
CAP = 2
NBLK = 512
SLOTS = 1024
N_DP = 64
N_TENSOR = 8


def draw_gradient(key, part):
    key = jax.random.fold_in(key, 11)
    subkeys = jax.random.split(key, 7)
    row_scale = jnp.exp(jax.random.uniform(subkeys[0], (NBLK, BLK, 1), minval=0.0, maxval=math.log(3.2)))
    col_scale = jnp.exp(jax.random.uniform(subkeys[1], (NBLK, 1, BLK), minval=0.0, maxval=math.log(3.2)))
    row_pos = jnp.arange(BLK, dtype=jnp.float32).reshape(1, BLK, 1)
    row_ramp = jnp.sqrt(1.0 + 2.0 * row_pos / (BLK - 1))
    half_count = NBLK // 2
    within = (jnp.arange(NBLK) % half_count).astype(jnp.float32).reshape(NBLK, 1, 1)
    block_ramp = jnp.sqrt(1.0 + 2.0 * within / (half_count - 1))
    noise_part = jax.random.truncated_normal(subkeys[2], -4.0, 4.0, (NBLK, BLK, BLK))
    left_dirs = jax.random.truncated_normal(subkeys[4], -3.0, 3.0, (3, NBLK, BLK, 1))
    right_dirs = jax.random.truncated_normal(subkeys[5], -3.0, 3.0, (3, NBLK, 1, BLK))
    amp_noise = jnp.exp(jax.random.uniform(subkeys[6], (3, NBLK, 1, 1), minval=0.0, maxval=math.log(1.6)))
    strengths = (2.0, 1.2, 0.7)
    leading = jnp.zeros((NBLK, BLK, BLK), jnp.float32)
    for term in range(3):
        weight = strengths[term] * amp_noise[term] * BLK ** (-0.25)
        leading = leading + weight * left_dirs[term] * right_dirs[term]
    values = (0.3 * noise_part * row_scale * col_scale + leading) * row_ramp * block_ramp
    return values.reshape(NBLK, BLK * BLK).astype(jnp.bfloat16)


def draw_owner_table(key, part):
    key = jax.random.fold_in(key, 37)
    subkeys = jax.random.split(key, 2)
    devices = N_DP * N_TENSOR
    owners = jax.random.permutation(subkeys[0], devices).astype(jnp.int32)
    quarter = devices // 4
    busy_owners = jnp.tile(owners[:quarter], CAP)
    light_owners = jnp.tile(owners[quarter:3 * quarter], CAP // 2)
    listing = jnp.concatenate([busy_owners, light_owners])
    return jax.random.permutation(subkeys[1], listing).astype(jnp.int32)


def draw_prev_stats(key, part):
    key = jax.random.fold_in(key, 23)
    subkeys = jax.random.split(key, 2)
    spread = jax.random.uniform(subkeys[0], (SLOTS, 2, BLK, BLK), minval=-1.0, maxval=1.0)
    spread = 0.5 * (spread + jnp.swapaxes(spread, 2, 3))
    weights = jnp.exp(jax.random.uniform(subkeys[1], (SLOTS, 2, BLK), minval=0.0, maxval=math.log(16.0)))
    diagonal = BLK * weights
    smaller = jnp.minimum(diagonal[..., :, None], diagonal[..., None, :])
    off_part = 0.9 * spread * smaller / BLK
    on_diagonal = jnp.eye(BLK, dtype=bool)
    return jnp.where(on_diagonal, diagonal[..., None], off_part).astype(jnp.bfloat16)


def setup_inputs(seed: int = 0) -> dict:
    arg_keys = jax.random.split(jax.random.key(seed), 4)
    gradient = draw_gradient(jax.random.fold_in(arg_keys[3], 71), 0)
    owner_table = draw_owner_table(jax.random.fold_in(arg_keys[3], 71), 0)
    prev_stats = draw_prev_stats(jax.random.fold_in(arg_keys[3], 71), 0)
    return dict(gradient=gradient, owner_table=owner_table, prev_stats=prev_stats)


DECAY = 0.9
GRAFT_EPS = 1e-06

def owner_rank(owner_table):
    block_count = owner_table.shape[0]
    positions = jnp.arange(block_count, dtype=jnp.int32)
    same_owner = owner_table[:, None] == owner_table[None, :]
    earlier = positions[None, :] < positions[:, None]
    return lax.optimization_barrier(jnp.sum(jnp.where(same_owner & earlier, 1, 0), axis=1)).astype(jnp.int32)

def inverse_root(statistic):
    size = statistic.shape[0]
    identity = jnp.eye(size, dtype=jnp.float32)
    norm_scale = jnp.sqrt(jnp.sum(statistic * statistic))
    matrix = statistic / norm_scale
    root_est = identity
    for sweep in range(ITERS):
        factor = (5.0 * identity - matrix) * 0.25
        if sweep == 0:
            root_est = norm_scale ** (-0.25) * factor
        else:
            root_est = jnp.dot(root_est.astype(jnp.bfloat16), factor.astype(jnp.bfloat16), preferred_element_type=jnp.float32)
        if sweep + 1 < ITERS:
            factor_low = factor.astype(jnp.bfloat16)
            square = jnp.dot(factor_low, factor_low, preferred_element_type=jnp.float32)
            square_low = square.astype(jnp.bfloat16)
            fourth = jnp.dot(square_low, square_low, preferred_element_type=jnp.float32)
            matrix = jnp.dot(fourth.astype(jnp.bfloat16), matrix.astype(jnp.bfloat16), preferred_element_type=jnp.float32)
    return root_est

def precondition(block_matrix, saved):
    left_stat = DECAY * saved[0].astype(jnp.float32) + jnp.dot(block_matrix, block_matrix.T, preferred_element_type=jnp.float32)
    right_stat = DECAY * saved[1].astype(jnp.float32) + jnp.dot(block_matrix.T, block_matrix, preferred_element_type=jnp.float32)
    left_root = inverse_root(left_stat).astype(jnp.bfloat16)
    right_root = inverse_root(right_stat).astype(jnp.bfloat16)
    middle = jnp.dot(block_matrix, right_root, preferred_element_type=jnp.float32).astype(jnp.bfloat16)
    return jnp.dot(left_root, middle, preferred_element_type=jnp.float32).astype(jnp.bfloat16)

def reference(gradient, owner_table, prev_stats):
    slot_rank = owner_rank(owner_table)
    slot_index = (owner_table * CAP + slot_rank).astype(jnp.int32)
    blocks = gradient.reshape(NBLK, BLK, BLK)

    def per_block(block_index):
        return precondition(blocks[block_index], prev_stats[slot_index[block_index]])
    updates = lax.map(per_block, jnp.arange(NBLK, dtype=jnp.int32))
    half_count = NBLK // 2
    grad_sq = lax.optimization_barrier(jnp.sum(jnp.square(gradient.astype(jnp.float32)), axis=1))
    update_sq = lax.optimization_barrier(jnp.sum(jnp.square(updates.astype(jnp.float32)), axis=(1, 2)))
    grad_layers = lax.optimization_barrier(jnp.sum(grad_sq.reshape(2, half_count), axis=1))
    update_layers = lax.optimization_barrier(jnp.sum(update_sq.reshape(2, half_count), axis=1))
    graft_ratio = jnp.sqrt(grad_layers / (update_layers + GRAFT_EPS))
    per_row = jnp.repeat(graft_ratio, half_count)
    scaled = updates.astype(jnp.float32) * per_row[:, None, None]
    return scaled.astype(jnp.bfloat16).reshape(NBLK, BLK * BLK)
```

```python
import jax
import jax.numpy as jnp
from jax import lax
from jax.experimental import pallas as pl
from jax.experimental.pallas import tpu as pltpu
from jax.sharding import PartitionSpec as P

BLK = 512
ITERS = 2
DECAY = 0.9
GRAFT_EPS = 1e-06

NZ = 16
NQ = 4
NT = 8
NP = NQ * NT
CAP1 = 16

MESH = pl.DeviceIdType.MESH
F32 = jnp.float32
BF16 = jnp.bfloat16


def batched_product(first, second):
    return jnp.einsum("...ij,...jk->...ik", first, second, preferred_element_type=F32)


def owner_rank(owner_table):
    block_count = owner_table.shape[0]
    positions = jnp.arange(block_count, dtype=jnp.int32)
    same_owner = owner_table[:, None] == owner_table[None, :]
    earlier = positions[None, :] < positions[:, None]
    return jnp.sum(jnp.where(same_owner & earlier, 1, 0), axis=1).astype(jnp.int32)


def inverse_roots(statistic):
    identity = jnp.eye(statistic.shape[-1], dtype=F32)
    norm_scale = jnp.sqrt(jnp.sum(statistic * statistic, axis=(-2, -1), keepdims=True))
    matrix = statistic / norm_scale
    root_est = statistic
    for sweep in range(ITERS):
        factor = (5.0 * identity - matrix) * 0.25
        if sweep == 0:
            root_est = norm_scale ** (-0.25) * factor
        else:
            root_est = batched_product(root_est.astype(BF16), factor.astype(BF16))
        if sweep + 1 < ITERS:
            factor_low = factor.astype(BF16)
            square_low = batched_product(factor_low, factor_low).astype(BF16)
            fourth = batched_product(square_low, square_low)
            matrix = batched_product(fourth.astype(BF16), matrix.astype(BF16))
    return root_est


def precondition(block_matrix, saved):
    left_gram = jnp.einsum("cij,ckj->cik", block_matrix, block_matrix, preferred_element_type=F32)
    right_gram = jnp.einsum("cji,cjk->cik", block_matrix, block_matrix, preferred_element_type=F32)
    statistic = DECAY * saved.astype(F32) + jnp.stack([left_gram, right_gram], axis=1)
    roots = inverse_roots(statistic).astype(BF16)
    middle = batched_product(block_matrix, roots[:, 1]).astype(BF16)
    return batched_product(roots[:, 0], middle).astype(BF16)


def general_program(gradient, owner_table, prev_stats):
    dp_size = lax.axis_size("dp")
    tensor_size = lax.axis_size("tensor")
    devices = dp_size * tensor_size
    capacity = prev_stats.shape[0]
    block_count, entries = gradient.shape
    slot_rank = owner_rank(owner_table)
    positions = jnp.arange(block_count, dtype=jnp.int32)
    inverse = (
        jnp.zeros((capacity * devices,), jnp.int32)
        .at[slot_rank * devices + owner_table]
        .set(positions)
    )
    outgoing = jnp.take(gradient, inverse, axis=0).reshape(capacity, dp_size, tensor_size, entries)

    def exchange(rows):
        rows = lax.all_to_all(rows, "dp", split_axis=1, concat_axis=1, tiled=True)
        return lax.all_to_all(rows, "tensor", split_axis=2, concat_axis=2, tiled=True)

    received = exchange(outgoing)
    updates = precondition(received.reshape(capacity, BLK, BLK), prev_stats)
    returned = exchange(updates.reshape(capacity, dp_size, tensor_size, entries))
    flat_back = returned.reshape(capacity * devices, entries)
    mine = jnp.take(flat_back, slot_rank * devices + owner_table, axis=0)
    half_count = block_count // 2
    grad_sq = jnp.sum(
        jnp.sum(jnp.square(gradient.astype(F32)), axis=1).reshape(2, half_count), axis=1
    )
    update_sq = jnp.sum(
        jnp.sum(jnp.square(mine.astype(F32)), axis=1).reshape(2, half_count), axis=1
    )
    grad_total, update_total = lax.psum((grad_sq, update_sq), ("dp", "tensor"))
    graft_ratio = jnp.sqrt(grad_total / (update_total + GRAFT_EPS))
    per_row = jnp.where(positions < half_count, graft_ratio[0], graft_ratio[1])
    return (mine.astype(F32) * per_row[:, None]).astype(BF16)


def iota(shape, dim):
    return lax.broadcasted_iota(jnp.int32, shape, dim)


def ones_where(mask):
    return jnp.where(mask, 1.0, 0.0)


def dot(a, b):
    return jnp.dot(a, b, preferred_element_type=F32)


def dot_t(a, b):
    return lax.dot_general(a, b, (((1,), (1,)), ((), ())), preferred_element_type=F32)


def kernel(
    grad_ref,
    owner_ref,
    stats_ref,
    out_ref,
    flag_ref,
    stats_v,
    stat_sem,
    za_send, za_recv, zb_send, zb_recv,
    pa_send, pa_recv, pb_send, pb_recv,
    ra_send, ra_recv, rb_send, rb_recv,
    ya_send, ya_recv, yb_send, yb_recv,
    norm_mine, norm_plane, plane_mine, plane_all,
    fold_ref, unfold_ref, ohm_ref, ohmt_ref, fin0_ref, fin1_ref,
    block_ref, root_ref,
    z_ssem, z_rsem, p_ssem, p_rsem,
):
    dp = lax.axis_index("dp")
    t = lax.axis_index("tensor")
    z = dp // NQ
    q = lax.rem(dp, NQ)
    p = q * NT + t
    me = z * NP + p

    stat_copy = pltpu.make_async_copy(stats_ref, stats_v, stat_sem)
    stat_copy.start()

    def z_peer(k):
        half = k // 2
        off = jnp.where(lax.rem(k, 2) == 0, 8 + half, 8 - half)
        return off, lax.rem(z + off, NZ)

    def p_peer(k):
        return lax.rem(p + k, NP)

    barrier = pltpu.get_barrier_semaphore()

    def greet_z(k, c):
        _, zt = z_peer(k)
        pl.semaphore_signal(barrier, inc=1, device_id=(zt * NQ + q, t), device_id_type=MESH)
        return c

    def greet_p(k, c):
        pt = p_peer(k)
        pl.semaphore_signal(
            barrier, inc=1, device_id=(z * NQ + pt // NT, lax.rem(pt, NT)), device_id_type=MESH
        )
        return c

    lax.fori_loop(1, NZ, greet_z, 0)
    lax.fori_loop(1, NP, greet_p, 0)

    def z_copy(phase, k, src, dst, whole):
        off, zt = z_peer(k)
        return pltpu.make_async_remote_copy(
            src_ref=src if whole else src.at[zt],
            dst_ref=dst.at[z],
            send_sem=z_ssem.at[phase, off],
            recv_sem=z_rsem.at[phase, off],
            device_id=(zt * NQ + q, t),
            device_id_type=MESH,
        )

    def p_copy(phase, k, src, dst, whole):
        pt = p_peer(k)
        return pltpu.make_async_remote_copy(
            src_ref=src if whole else src.at[pt],
            dst_ref=dst.at[p],
            send_sem=p_ssem.at[phase, k],
            recv_sem=p_rsem.at[phase, k],
            device_id=(z * NQ + pt // NT, lax.rem(pt, NT)),
            device_id_type=MESH,
        )

    def start(make, count, phase, src, dst, whole=False):
        def step(k, c):
            make(phase, k, src, dst, whole).start()
            return c

        lax.fori_loop(1, count, step, 0)
        if make is z_copy:
            dst[pl.ds(z, 1)] = src[...][None] if whole else src[pl.ds(z, 1)]
        else:
            dst[pl.ds(p, 1)] = src[...][None] if whole else src[pl.ds(p, 1)]

    def arrive(make, count, phase, src, dst, whole=False):
        def step(k, c):
            make(phase, k, src, dst, whole).wait_recv()
            return c

        lax.fori_loop(1, count, step, 0)

    def drain(make, count, phase, src, dst, whole=False):
        def step(k, c):
            make(phase, k, src, dst, whole).wait_send()
            return c

        lax.fori_loop(1, count, step, 0)

    n = BLK
    i0 = iota((n, n), 0)
    i1 = iota((n, n), 1)
    owner_row = owner_ref[...].astype(F32)
    owner_col = jnp.sum(jnp.where(i0 == i1, owner_row, 0.0), axis=1, keepdims=True)
    same = owner_col == owner_row
    rank_row = jnp.sum(ones_where(same & (i0 < i1)), axis=0, keepdims=True)
    rank_col = jnp.sum(ones_where(same & (i1 < i0)), axis=1, keepdims=True)
    plane_row = jnp.floor(owner_row * (1.0 / NP))
    plane_col = jnp.floor(owner_col * (1.0 / NP))
    second_row = jnp.where(rank_row > 0.5, plane_row, -1.0)
    second_col = jnp.where(rank_col > 0.5, plane_col, -2.0)
    second_col_b = jnp.where(rank_col > 0.5, plane_col, -1.0)
    second_row_b = jnp.where(rank_row > 0.5, plane_row, -2.0)
    pos_row = jnp.sum(ones_where((second_col == second_row) & (i0 < i1)), axis=0, keepdims=True)
    pos_col = jnp.sum(ones_where((second_col_b == second_row_b) & (i1 < i0)), axis=1, keepdims=True)

    first_row = jnp.where(rank_row < 0.5, owner_row, -1.0)
    first_col = jnp.where(rank_col < 0.5, owner_col, -1.0)
    late_row = jnp.where(
        (rank_row > 0.5) & (pos_row < CAP1 - 0.5), plane_row * CAP1 + pos_row, -1.0
    )
    late_col = jnp.where(
        (rank_col > 0.5) & (pos_col < CAP1 - 0.5), plane_col * CAP1 + pos_col, -1.0
    )
    f0 = i0.astype(F32)
    f1 = i1.astype(F32)

    pick1 = ones_where(late_row == f0[: NZ * CAP1]).astype(BF16)
    zb_send[...] = dot(pick1, grad_ref[...]).astype(BF16).reshape(NZ, CAP1, n)
    pick0 = ones_where(first_row == f0).astype(BF16)
    za_send[...] = dot(pick0, grad_ref[...]).astype(BF16).reshape(NZ, NP, n)

    pl.semaphore_wait(barrier, NZ - 1 + NP - 1)
    start(z_copy, NZ, 0, zb_send, zb_recv)
    start(z_copy, NZ, 1, za_send, za_recv)

    fin0_ref[...] = ones_where(first_col == f1).astype(BF16)
    fin1_ref[...] = ones_where(late_col == f1[:, : NZ * CAP1]).astype(BF16)
    overflow = jnp.max(jnp.where(rank_row > 0.5, pos_row, 0.0), axis=1, keepdims=True)
    flag_ref[...] = jnp.broadcast_to(overflow, flag_ref.shape)

    to_zp = (i0 & (NZ - 1)) * NP + lax.shift_right_logical(i0, 4)
    to_zp_t = (i1 & (NZ - 1)) * NP + lax.shift_right_logical(i1, 4)
    fold_ref[...] = ones_where(to_zp == i1).astype(BF16)
    unfold_ref[...] = ones_where(to_zp_t == i0).astype(BF16)

    z_base = (z * NP).astype(F32)
    dev_of = z_base + lax.shift_right_logical(i0, 4).astype(F32)
    dev_of_t = z_base + lax.shift_right_logical(i1, 4).astype(F32)
    held_row = jnp.where(rank_row > 0.5, owner_row, -1.0)
    held_col = jnp.where(rank_col > 0.5, owner_col, -1.0)
    at_col = jnp.sum(jnp.where(held_row == dev_of, pos_row + 1.0, 0.0), axis=1, keepdims=True)
    at_row = jnp.sum(jnp.where(held_col == dev_of_t, pos_col + 1.0, 0.0), axis=0, keepdims=True)
    m = NZ * CAP1
    a0, a1 = iota((n, m), 0), iota((n, m), 1)
    ohm_ref[...] = ones_where(
        (lax.shift_right_logical(a1, 4) == (a0 & (NZ - 1)))
        & ((a1 & (CAP1 - 1)).astype(F32) == at_col - 1.0)
    ).astype(BF16)
    c0, c1 = iota((m, n), 0), iota((m, n), 1)
    ohmt_ref[...] = ones_where(
        (lax.shift_right_logical(c0, 4) == (c1 & (NZ - 1)))
        & ((c0 & (CAP1 - 1)).astype(F32) == at_row - 1.0)
    ).astype(BF16)

    me_f = me.astype(F32)
    lane = iota((1, n), 1)

    def slot_facts(slot):
        here = (owner_row == me_f) & (jnp.abs(rank_row - slot) < 0.5)
        used = jnp.sum(ones_where(here), axis=1, keepdims=True)
        layer1 = jnp.sum(ones_where(here & (lane >= n // 2)), axis=1, keepdims=True)
        return used, layer1

    identity5 = jnp.where(i0 == i1, 1.25, 0.0)

    def inverse_root(stat):
        total = jnp.sum(jnp.sum(stat * stat, axis=1, keepdims=True), axis=0, keepdims=True)
        norm_scale = jnp.sqrt(total)
        matrix = stat * (1.0 / norm_scale)
        factor = identity5 - 0.25 * matrix
        low = factor.astype(BF16)
        root = (lax.rsqrt(jnp.sqrt(norm_scale)) * factor).astype(BF16)
        square = dot(low, low).astype(BF16)
        fourth = dot(square, square).astype(BF16)
        matrix = dot(fourth, matrix.astype(BF16))
        factor = (identity5 - 0.25 * matrix).astype(BF16)
        return dot(root, factor).astype(BF16)

    def owner_work(slot, incoming, outgoing):
        block = dot(unfold_ref[...], incoming[...].reshape(n, n)).astype(BF16)
        block_ref[...] = block
        eye = ones_where(i0 == i1).astype(BF16)
        block_t = dot_t(eye, block).astype(BF16)
        right = inverse_root(DECAY * stats_v[slot, 1].astype(F32) + dot_t(block_t, block_t))
        middle = dot(block_ref[...], right).astype(BF16)
        left = inverse_root(
            DECAY * stats_v[slot, 0].astype(F32) + dot_t(block_ref[...], block_ref[...])
        )
        raw = dot(left, middle)
        used, layer1 = slot_facts(slot)
        raw = jnp.where(used > 0.5, raw, 0.0).astype(BF16)
        root_ref[...] = raw
        outgoing[...] = dot(fold_ref[...], root_ref[...]).astype(BF16).reshape(NP, NZ, n)
        raw_f = root_ref[...].astype(F32)
        update_sq = jnp.sum(jnp.sum(raw_f * raw_f, axis=1, keepdims=True), axis=0, keepdims=True)
        block_f = block_ref[...].astype(F32)
        grad_sq = jnp.sum(jnp.sum(block_f * block_f, axis=1, keepdims=True), axis=0, keepdims=True)
        g1 = jnp.where(layer1 > 0.5, grad_sq, 0.0)
        u1 = jnp.where(layer1 > 0.5, update_sq, 0.0)
        return grad_sq - g1, g1, update_sq - u1, u1

    arrive(z_copy, NZ, 0, zb_send, zb_recv)
    pb_send[...] = dot(ohm_ref[...], zb_recv[...].reshape(m, n)).astype(BF16).reshape(NP, NZ, n)
    start(p_copy, NP, 0, pb_send, pb_recv)
    stat_copy.wait()
    arrive(p_copy, NP, 0, pb_send, pb_recv)
    sums1 = owner_work(1, pb_recv, rb_send)
    start(p_copy, NP, 2, rb_send, rb_recv)

    arrive(z_copy, NZ, 1, za_send, za_recv)
    pa_send[...] = dot(fold_ref[...], za_recv[...].reshape(n, n)).astype(BF16).reshape(NP, NZ, n)
    start(p_copy, NP, 1, pa_send, pa_recv)

    arrive(p_copy, NP, 2, rb_send, rb_recv)
    yb_send[...] = dot(ohmt_ref[...], rb_recv[...].reshape(n, n)).astype(BF16).reshape(NZ, CAP1, n)
    start(z_copy, NZ, 2, yb_send, yb_recv)

    arrive(p_copy, NP, 1, pa_send, pa_recv)
    sums0 = owner_work(0, pa_recv, ra_send)
    start(p_copy, NP, 3, ra_send, ra_recv)
    s0 = iota((8, 128), 0)
    tile = jnp.zeros((8, 128), F32)
    for r in range(4):
        tile = jnp.where(s0 == r, sums0[r] + sums1[r], tile)
    norm_mine[...] = tile
    start(p_copy, NP, 4, norm_mine, norm_plane, whole=True)

    arrive(p_copy, NP, 3, ra_send, ra_recv)
    ya_send[...] = dot(unfold_ref[...], ra_recv[...].reshape(n, n)).astype(BF16).reshape(NZ, NP, n)
    start(z_copy, NZ, 3, ya_send, ya_recv)

    arrive(p_copy, NP, 4, norm_mine, norm_plane, whole=True)
    plane_mine[...] = jnp.sum(norm_plane[...], axis=0)
    start(z_copy, NZ, 4, plane_mine, plane_all, whole=True)

    arrive(z_copy, NZ, 2, yb_send, yb_recv)
    late = dot(fin1_ref[...], yb_recv[...].reshape(m, n))
    arrive(z_copy, NZ, 4, plane_mine, plane_all, whole=True)
    totals = jnp.sum(plane_all[...], axis=0)
    ratio0 = jnp.sqrt(totals[0:1, 0:1] / (totals[2:3, 0:1] + GRAFT_EPS))
    ratio1 = jnp.sqrt(totals[1:2, 0:1] / (totals[3:4, 0:1] + GRAFT_EPS))
    ratio = jnp.where(iota((n, 1), 0) < n // 2, ratio0, ratio1)
    arrive(z_copy, NZ, 3, ya_send, ya_recv)
    rows = dot(fin0_ref[...], ya_recv[...].reshape(n, n)) + late
    out_ref[...] = (rows * ratio).astype(BF16)

    drain(z_copy, NZ, 0, zb_send, zb_recv)
    drain(z_copy, NZ, 1, za_send, za_recv)
    drain(z_copy, NZ, 2, yb_send, yb_recv)
    drain(z_copy, NZ, 3, ya_send, ya_recv)
    drain(z_copy, NZ, 4, plane_mine, plane_all, whole=True)
    drain(p_copy, NP, 0, pb_send, pb_recv)
    drain(p_copy, NP, 1, pa_send, pa_recv)
    drain(p_copy, NP, 2, rb_send, rb_recv)
    drain(p_copy, NP, 3, ra_send, ra_recv)
    drain(p_copy, NP, 4, norm_mine, norm_plane, whole=True)


def fast_program(gradient, owner_table, prev_stats):
    n = BLK
    za, zb = pltpu.VMEM((NZ, NP, n), BF16), pltpu.VMEM((NZ, CAP1, n), BF16)
    pp = pltpu.VMEM((NP, NZ, n), BF16)
    square = pltpu.VMEM((n, n), BF16)
    vmem = pl.BlockSpec(memory_space=pltpu.VMEM)
    return pl.pallas_call(
        kernel,
        out_shape=(
            jax.ShapeDtypeStruct((n, n), BF16),
            jax.ShapeDtypeStruct((8, 128), F32),
        ),
        in_specs=[vmem, vmem, pl.BlockSpec(memory_space=pl.ANY)],
        out_specs=(vmem, vmem),
        scratch_shapes=[
            pltpu.VMEM((2, 2, n, n), BF16),
            pltpu.SemaphoreType.DMA,
            za, za, zb, zb,
            pp, pp, pp, pp,
            pp, pp, pp, pp,
            za, za, zb, zb,
            pltpu.VMEM((8, 128), F32),
            pltpu.VMEM((NP, 8, 128), F32),
            pltpu.VMEM((8, 128), F32),
            pltpu.VMEM((NZ, 8, 128), F32),
            square, square,
            pltpu.VMEM((n, NZ * CAP1), BF16),
            pltpu.VMEM((NZ * CAP1, n), BF16),
            square,
            pltpu.VMEM((n, NZ * CAP1), BF16),
            square, square,
            pltpu.SemaphoreType.DMA((5, NZ)),
            pltpu.SemaphoreType.DMA((5, NZ)),
            pltpu.SemaphoreType.DMA((5, NP)),
            pltpu.SemaphoreType.DMA((5, NP)),
        ],
        compiler_params=pltpu.CompilerParams(
            collective_id=0, has_side_effects=True, vmem_limit_bytes=56 << 20
        ),
    )(gradient, owner_table.reshape(1, -1), prev_stats)


def on_device(gradient, owner_table, prev_stats):
    update, overflow = fast_program(gradient, owner_table, prev_stats)
    return lax.cond(
        overflow[0, 0] > CAP1 - 0.5,
        lambda g, o, s, u: general_program(g, o, s),
        lambda g, o, s, u: u,
        gradient,
        owner_table,
        prev_stats,
        update,
    )


def solution(mesh):
    in_specs = (P(None, ("dp", "tensor")), P(), P(("dp", "tensor"), None, None, None))
    out_specs = P(None, ("dp", "tensor"))
    return jax.shard_map(
        on_device, mesh=mesh, in_specs=in_specs, out_specs=out_specs, check_vma=False
    )
```

```python
import jax
import jax.numpy as jnp
from jax import lax
from jax.experimental import pallas as pl
from jax.experimental.pallas import tpu as pltpu
from jax.sharding import PartitionSpec as P

BLK = 512
ITERS = 2
DECAY = 0.9
GRAFT_EPS = 1e-06

NZ = 16
NQ = 4
NT = 8
NP = NQ * NT
HALF = 16
CAP1 = 16

MESH = pl.DeviceIdType.MESH
F32 = jnp.float32
BF16 = jnp.bfloat16


def batched_product(first, second):
    return jnp.einsum("...ij,...jk->...ik", first, second, preferred_element_type=F32)


def owner_rank(owner_table):
    block_count = owner_table.shape[0]
    positions = jnp.arange(block_count, dtype=jnp.int32)
    same_owner = owner_table[:, None] == owner_table[None, :]
    earlier = positions[None, :] < positions[:, None]
    return jnp.sum(jnp.where(same_owner & earlier, 1, 0), axis=1).astype(jnp.int32)


def inverse_roots(statistic):
    identity = jnp.eye(statistic.shape[-1], dtype=F32)
    norm_scale = jnp.sqrt(jnp.sum(statistic * statistic, axis=(-2, -1), keepdims=True))
    matrix = statistic / norm_scale
    root_est = statistic
    for sweep in range(ITERS):
        factor = (5.0 * identity - matrix) * 0.25
        if sweep == 0:
            root_est = norm_scale ** (-0.25) * factor
        else:
            root_est = batched_product(root_est.astype(BF16), factor.astype(BF16))
        if sweep + 1 < ITERS:
            factor_low = factor.astype(BF16)
            square_low = batched_product(factor_low, factor_low).astype(BF16)
            fourth = batched_product(square_low, square_low)
            matrix = batched_product(fourth.astype(BF16), matrix.astype(BF16))
    return root_est


def precondition(block_matrix, saved):
    left_gram = jnp.einsum("cij,ckj->cik", block_matrix, block_matrix, preferred_element_type=F32)
    right_gram = jnp.einsum("cji,cjk->cik", block_matrix, block_matrix, preferred_element_type=F32)
    statistic = DECAY * saved.astype(F32) + jnp.stack([left_gram, right_gram], axis=1)
    roots = inverse_roots(statistic).astype(BF16)
    middle = batched_product(block_matrix, roots[:, 1]).astype(BF16)
    return batched_product(roots[:, 0], middle).astype(BF16)


def general_program(gradient, owner_table, prev_stats):
    dp_size = lax.axis_size("dp")
    tensor_size = lax.axis_size("tensor")
    devices = dp_size * tensor_size
    capacity = prev_stats.shape[0]
    block_count, entries = gradient.shape
    slot_rank = owner_rank(owner_table)
    positions = jnp.arange(block_count, dtype=jnp.int32)
    inverse = (
        jnp.zeros((capacity * devices,), jnp.int32)
        .at[slot_rank * devices + owner_table]
        .set(positions)
    )
    outgoing = jnp.take(gradient, inverse, axis=0).reshape(capacity, dp_size, tensor_size, entries)

    def exchange(rows):
        rows = lax.all_to_all(rows, "dp", split_axis=1, concat_axis=1, tiled=True)
        return lax.all_to_all(rows, "tensor", split_axis=2, concat_axis=2, tiled=True)

    received = exchange(outgoing)
    updates = precondition(received.reshape(capacity, BLK, BLK), prev_stats)
    returned = exchange(updates.reshape(capacity, dp_size, tensor_size, entries))
    flat_back = returned.reshape(capacity * devices, entries)
    mine = jnp.take(flat_back, slot_rank * devices + owner_table, axis=0)
    half_count = block_count // 2
    grad_sq = jnp.sum(
        jnp.sum(jnp.square(gradient.astype(F32)), axis=1).reshape(2, half_count), axis=1
    )
    update_sq = jnp.sum(
        jnp.sum(jnp.square(mine.astype(F32)), axis=1).reshape(2, half_count), axis=1
    )
    grad_total, update_total = lax.psum((grad_sq, update_sq), ("dp", "tensor"))
    graft_ratio = jnp.sqrt(grad_total / (update_total + GRAFT_EPS))
    per_row = jnp.where(positions < half_count, graft_ratio[0], graft_ratio[1])
    return (mine.astype(F32) * per_row[:, None]).astype(BF16)


def iota(shape, dim):
    return lax.broadcasted_iota(jnp.int32, shape, dim)


def ones_where(mask):
    return jnp.where(mask, 1.0, 0.0)


def dot(a, b):
    return jnp.dot(a, b, preferred_element_type=F32)


def dot_t(a, b):
    return lax.dot_general(a, b, (((1,), (1,)), ((), ())), preferred_element_type=F32)


def kernel(
    grad_hbm,
    owner_ref,
    stats_hbm,
    out_ref,
    flag_ref,
    grad_v, stats_v,
    z_out, z_in,
    pb_out, pb_in, pa_out, pa_in,
    rb_out, rb_in, ra_out, ra_in,
    y_out, y_in,
    norm_mine, norm_plane, plane_mine, plane_all,
    fold_ref, unfold_ref, fold_half, unfold_half, place_ref, place_t_ref, final_ref,
    block_ref, raw_ref, rows_ref,
    load_sem, z_ssem, z_rsem, p_ssem, p_rsem,
):
    dp = lax.axis_index("dp")
    t = lax.axis_index("tensor")
    z = dp // NQ
    q = lax.rem(dp, NQ)
    core = lax.rem(q, 2)
    p = q * NT + t
    j = (q // 2) * NT + t
    me = z * NP + p
    n = BLK
    m = NZ * HALF

    grad_copy = pltpu.make_async_copy(grad_hbm, grad_v, load_sem.at[0])
    stat_copy = pltpu.make_async_copy(stats_hbm, stats_v, load_sem.at[1])
    grad_copy.start()

    def z_peer(k):
        half = k // 2
        return lax.rem(z + jnp.where(lax.rem(k, 2) == 0, 8 + half, 8 - half), NZ)

    def z_id(zt):
        return (zt * NQ + q, t)

    def p_id(pt):
        return (z * NQ + pt // NT, lax.rem(pt, NT))

    def half_id(h, jt):
        return (z * NQ + (jt // NT) * 2 + h, lax.rem(jt, NT))

    barrier = pltpu.get_barrier_semaphore()

    def greet_z(k, c):
        pl.semaphore_signal(barrier, inc=1, device_id=z_id(z_peer(k)), device_id_type=MESH)
        return c

    def greet_p(k, c):
        pl.semaphore_signal(
            barrier, inc=1, device_id=p_id(lax.rem(p + k, NP)), device_id_type=MESH
        )
        return c

    lax.fori_loop(1, NZ, greet_z, 0)
    lax.fori_loop(1, NP, greet_p, 0)
    stat_copy.start()

    def remote(src, dst, ssem, rsem, device):
        return pltpu.make_async_remote_copy(
            src_ref=src, dst_ref=dst, send_sem=ssem, recv_sem=rsem,
            device_id=device, device_id_type=MESH,
        )

    def z_send(phase, src, dst):
        def step(k, c):
            zt = z_peer(k)
            remote(src.at[zt], dst.at[z], z_ssem.at[phase], z_rsem.at[phase], z_id(zt)).start()
            return c

        lax.fori_loop(1, NZ, step, 0)
        dst[pl.ds(z, 1)] = src[pl.ds(z, 1)]

    def z_wait(phase, dst):
        part = dst.at[pl.ds(0, NZ - 1)]
        remote(part, part, z_ssem.at[phase], z_rsem.at[phase], z_id(z)).wait_recv()

    def z_drain(phase, src):
        part = src.at[pl.ds(0, NZ - 1)]
        remote(part, part, z_ssem.at[phase], z_rsem.at[phase], z_id(z)).wait_send()

    def p_send(phase, src, dst):
        def step(k, c):
            pt = lax.rem(p + k, NP)
            remote(src.at[pt], dst.at[p], p_ssem.at[phase], p_rsem.at[phase], p_id(pt)).start()
            return c

        lax.fori_loop(1, NP, step, 0)
        dst[pl.ds(p, 1)] = src[pl.ds(p, 1)]

    def p_wait(phase, dst, count):
        part = dst.at[pl.ds(0, count)]
        remote(part, part, p_ssem.at[phase], p_rsem.at[phase], p_id(p)).wait_recv()

    def p_drain(phase, src, count):
        part = src.at[pl.ds(0, count)]
        remote(part, part, p_ssem.at[phase], p_rsem.at[phase], p_id(p)).wait_send()

    def to_half(phase, h, src, dst):
        def send(jt):
            remote(
                src.at[jt], dst.at[p], p_ssem.at[phase], p_rsem.at[phase], half_id(h, jt)
            ).start()

        def step(k, c):
            send(lax.rem(j + k, HALF))
            return c

        lax.fori_loop(1, HALF, step, 0)

        @pl.when(core != h)
        def _():
            send(j)

        @pl.when(core == h)
        def _():
            dst[pl.ds(p, 1)] = src[pl.ds(j, 1)]

    def to_half_drain(phase, h, src):
        @pl.when(core == h)
        def _():
            p_drain(phase, src, HALF - 1)

        @pl.when(core != h)
        def _():
            p_drain(phase, src, HALF)

    def from_half(phase, src, dst):
        def step(k, c):
            pt = lax.rem(p + k, NP)
            remote(src.at[pt], dst.at[j], p_ssem.at[phase], p_rsem.at[phase], p_id(pt)).start()
            return c

        lax.fori_loop(1, NP, step, 0)
        dst[pl.ds(j, 1)] = src[pl.ds(p, 1)]

    def from_half_wait(phase, h, dst):
        @pl.when(core == h)
        def _():
            p_wait(phase, dst, HALF - 1)

        @pl.when(core != h)
        def _():
            p_wait(phase, dst, HALF)

    i0 = iota((n, n), 0)
    i1 = iota((n, n), 1)
    owner_row_i = owner_ref[...]
    owner_row = owner_row_i.astype(F32)
    owner_col = jnp.sum(jnp.where(i0 == i1, owner_row, 0.0), axis=1, keepdims=True)
    owner_col_i = owner_col.astype(jnp.int32)
    same = owner_col == owner_row
    rank_row = jnp.sum(ones_where(same & (i0 < i1)), axis=0, keepdims=True)
    rank_col = jnp.sum(ones_where(same & (i1 < i0)), axis=1, keepdims=True)

    def first_key(owner):
        place = (lax.shift_right_logical(owner, 4) & 1) * NT + (owner & (NT - 1))
        chunk = 1 + (lax.shift_right_logical(owner, 3) & 1)
        return chunk * m + lax.shift_right_logical(owner, 5) * HALF + place

    plane_row = jnp.floor(owner_row * (1.0 / NP))
    plane_col = jnp.floor(owner_col * (1.0 / NP))
    pos_row = jnp.sum(
        ones_where(
            (jnp.where(rank_col > 0.5, plane_col, -2.0) == jnp.where(rank_row > 0.5, plane_row, -1.0))
            & (i0 < i1)
        ),
        axis=0,
        keepdims=True,
    )
    pos_col = jnp.sum(
        ones_where(
            (jnp.where(rank_col > 0.5, plane_col, -1.0) == jnp.where(rank_row > 0.5, plane_row, -2.0))
            & (i1 < i0)
        ),
        axis=1,
        keepdims=True,
    )

    def keys(owner_i, rank, plane, pos):
        second = jnp.where(pos < CAP1 - 0.5, plane * CAP1 + pos, -1.0)
        return jnp.where(rank > 0.5, second, first_key(owner_i).astype(F32))

    key_row = keys(owner_row_i, rank_row, plane_row, pos_row)
    key_col = keys(owner_col_i, rank_col, plane_col, pos_col)

    grad_copy.wait()
    h0 = iota((m, n), 0).astype(F32)
    for chunk in range(3):
        pick = ones_where(key_row == h0 + float(chunk * m)).astype(BF16)
        z_out[chunk] = dot(pick, grad_v[...]).astype(BF16).reshape(NZ, HALF, n)
        if chunk == 0:
            pl.semaphore_wait(barrier, NZ - 1 + NP - 1)
        z_send(chunk, z_out.at[chunk], z_in.at[chunk])

    final_ref[...] = ones_where(key_col == iota((n, 3 * m), 1).astype(F32)).astype(BF16)
    flag_ref[0, 0] = jnp.max(jnp.where(rank_row > 0.5, pos_row, 0.0))

    def fold_table(size, places):
        a, b = iota((size, size), 0), iota((size, size), 1)
        there = (a & (NZ - 1)) * places + lax.shift_right_logical(a, 4)
        back = (b & (NZ - 1)) * places + lax.shift_right_logical(b, 4)
        return ones_where(there == b).astype(BF16), ones_where(back == a).astype(BF16)

    fold_ref[...], unfold_ref[...] = fold_table(n, NP)
    fold_half[...], unfold_half[...] = fold_table(m, HALF)

    z_base = (z * NP).astype(F32)
    dev_of = z_base + lax.shift_right_logical(i0, 4).astype(F32)
    dev_of_t = z_base + lax.shift_right_logical(i1, 4).astype(F32)
    held_row = jnp.where(rank_row > 0.5, owner_row, -1.0)
    held_col = jnp.where(rank_col > 0.5, owner_col, -1.0)
    at_col = jnp.sum(jnp.where(held_row == dev_of, pos_row + 1.0, 0.0), axis=1, keepdims=True)
    at_row = jnp.sum(jnp.where(held_col == dev_of_t, pos_col + 1.0, 0.0), axis=0, keepdims=True)
    a0, a1 = iota((n, m), 0), iota((n, m), 1)
    place_ref[...] = ones_where(
        (lax.shift_right_logical(a1, 4) == (a0 & (NZ - 1)))
        & ((a1 & (CAP1 - 1)).astype(F32) == at_col - 1.0)
    ).astype(BF16)
    c0, c1 = iota((m, n), 0), iota((m, n), 1)
    place_t_ref[...] = ones_where(
        (lax.shift_right_logical(c0, 4) == (c1 & (NZ - 1)))
        & ((c0 & (CAP1 - 1)).astype(F32) == at_row - 1.0)
    ).astype(BF16)
    norm_mine[...] = jnp.zeros_like(norm_mine)

    me_f = me.astype(F32)
    lane = iota((1, n), 1)
    identity5 = jnp.where(i0 == i1, 1.25, 0.0)

    def all_sum(x):
        return jnp.sum(jnp.sum(x, axis=1, keepdims=True), axis=0, keepdims=True)

    def inverse_root(stat):
        norm_scale = jnp.sqrt(all_sum(stat * stat))
        matrix = stat * (1.0 / norm_scale)
        factor = identity5 - 0.25 * matrix
        low = factor.astype(BF16)
        root = (lax.rsqrt(jnp.sqrt(norm_scale)) * factor).astype(BF16)
        square = dot(low, low).astype(BF16)
        fourth = dot(square, square).astype(BF16)
        matrix = dot(fourth, matrix.astype(BF16))
        factor = (identity5 - 0.25 * matrix).astype(BF16)
        return dot(root, factor).astype(BF16)

    def owner_work(slot, incoming, outgoing):
        block = dot(unfold_ref[...], incoming[...].reshape(n, n)).astype(BF16)
        block_ref[...] = block
        eye = ones_where(i0 == i1).astype(BF16)
        block_t = dot_t(eye, block).astype(BF16)
        right = inverse_root(DECAY * stats_v[slot, 1].astype(F32) + dot_t(block_t, block_t))
        middle = dot(block_ref[...], right).astype(BF16)
        left = inverse_root(
            DECAY * stats_v[slot, 0].astype(F32) + dot_t(block_ref[...], block_ref[...])
        )
        raw = dot(left, middle)
        here = (owner_row == me_f) & (jnp.abs(rank_row - float(slot)) < 0.5)
        used = all_sum(ones_where(here))
        layer1 = all_sum(ones_where(here & (lane >= n // 2)))
        raw_ref[...] = jnp.where(used > 0.5, raw, 0.0).astype(BF16)
        outgoing[...] = dot(fold_ref[...], raw_ref[...]).astype(BF16).reshape(NP, NZ, n)

        def tally():
            raw_f = raw_ref[...].astype(F32)
            block_f = block_ref[...].astype(F32)
            layer = jnp.where(layer1 > 0.5, 1, 0)
            s0 = iota((8, 128), 0)
            sums = jnp.where(s0 == layer, all_sum(block_f * block_f), 0.0)
            sums = sums + jnp.where(s0 == layer + 2, all_sum(raw_f * raw_f), 0.0)
            norm_mine[...] = norm_mine[...] + sums

        return tally

    z_wait(0, z_in.at[0])
    pb_out[...] = dot(place_ref[...], z_in[0].reshape(m, n)).astype(BF16).reshape(NP, NZ, n)
    p_send(0, pb_out, pb_in)

    def fold_in(h):
        z_wait(1 + h, z_in.at[1 + h])
        rows = dot(fold_half[...], z_in[1 + h].reshape(m, n)).astype(BF16)
        pa_out[h] = rows.reshape(HALF, NZ, n)
        to_half(1 + h, h, pa_out.at[h], pa_in)

    def fold_out(h):
        from_half_wait(4 + h, h, ra_in.at[h])
        rows = dot(unfold_half[...], ra_in[h].reshape(m, n)).astype(BF16)
        y_out[1 + h] = rows.reshape(NZ, HALF, n)
        z_send(4 + h, y_out.at[1 + h], y_in.at[1 + h])

    def first_work(h):
        @pl.when(core == h)
        def _():
            p_wait(1 + h, pa_in, NP - 1)
            tally = owner_work(0, pa_in, ra_out)
            from_half(4 + h, ra_out, ra_in.at[h])
            tally()

    fold_in(0)
    stat_copy.wait()
    p_wait(0, pb_in, NP - 1)
    tally = owner_work(1, pb_in, rb_out)
    p_send(3, rb_out, rb_in)
    tally()
    fold_in(1)
    first_work(0)

    p_wait(3, rb_in, NP - 1)
    rows = dot(place_t_ref[...], rb_in[...].reshape(n, n)).astype(BF16)
    y_out[0] = rows.reshape(NZ, HALF, n)
    z_send(3, y_out.at[0], y_in.at[0])

    first_work(1)

    def norm_step(k, c):
        pt = lax.rem(p + k, NP)
        remote(norm_mine, norm_plane.at[p], p_ssem.at[6], p_rsem.at[6], p_id(pt)).start()
        return c

    lax.fori_loop(1, NP, norm_step, 0)
    norm_plane[pl.ds(p, 1)] = norm_mine[...][None]

    fold_out(0)

    p_wait(6, norm_plane, NP - 1)
    plane_mine[...] = jnp.sum(norm_plane[...], axis=0)

    def plane_step(k, c):
        zt = z_peer(k)
        remote(plane_mine, plane_all.at[z], z_ssem.at[6], z_rsem.at[6], z_id(zt)).start()
        return c

    lax.fori_loop(1, NZ, plane_step, 0)
    plane_all[pl.ds(z, 1)] = plane_mine[...][None]

    fold_out(1)

    def returned(chunk):
        z_wait(3 + chunk, y_in.at[chunk])
        return dot(final_ref[:, chunk * m : (chunk + 1) * m], y_in[chunk].reshape(m, n))

    rows_ref[...] = returned(0)
    rows_ref[...] = rows_ref[...] + returned(1)
    z_wait(6, plane_all)
    totals = jnp.sum(plane_all[...], axis=0)
    ratio0 = jnp.sqrt(totals[0:1, 0:1] / (totals[2:3, 0:1] + GRAFT_EPS))
    ratio1 = jnp.sqrt(totals[1:2, 0:1] / (totals[3:4, 0:1] + GRAFT_EPS))
    ratio = jnp.where(iota((n, 1), 0) < n // 2, ratio0, ratio1)
    out_ref[...] = ((rows_ref[...] + returned(2)) * ratio).astype(BF16)

    for chunk in range(3):
        z_drain(chunk, z_out.at[chunk])
        z_drain(3 + chunk, y_out.at[chunk])
    z_drain(6, plane_all)
    p_drain(0, pb_out, NP - 1)
    p_drain(3, rb_out, NP - 1)
    p_drain(6, norm_plane, NP - 1)
    for h in range(2):
        to_half_drain(1 + h, h, pa_out.at[h])

        @pl.when(core == h)
        def _():
            p_drain(4 + h, ra_out, NP - 1)


def fast_program(gradient, owner_table, prev_stats):
    n = BLK
    m = NZ * HALF
    chunks = pltpu.VMEM((3, NZ, HALF, n), BF16)
    plane = pltpu.VMEM((NP, NZ, n), BF16)
    halves = pltpu.VMEM((2, HALF, NZ, n), BF16)
    square = pltpu.VMEM((n, n), BF16)
    vmem = pl.BlockSpec(memory_space=pltpu.VMEM)
    hbm = pl.BlockSpec(memory_space=pl.ANY)
    return pl.pallas_call(
        kernel,
        out_shape=(
            jax.ShapeDtypeStruct((n, n), BF16),
            jax.ShapeDtypeStruct((1, 1), F32),
        ),
        in_specs=[hbm, vmem, hbm],
        out_specs=(vmem, pl.BlockSpec(memory_space=pltpu.SMEM)),
        scratch_shapes=[
            square,
            pltpu.VMEM((2, 2, n, n), BF16),
            chunks, chunks,
            plane, plane, halves, plane,
            plane, plane, plane, halves,
            chunks, chunks,
            pltpu.VMEM((8, 128), F32),
            pltpu.VMEM((NP, 8, 128), F32),
            pltpu.VMEM((8, 128), F32),
            pltpu.VMEM((NZ, 8, 128), F32),
            square, square,
            pltpu.VMEM((m, m), BF16),
            pltpu.VMEM((m, m), BF16),
            pltpu.VMEM((n, m), BF16),
            pltpu.VMEM((m, n), BF16),
            pltpu.VMEM((n, 3 * m), BF16),
            square, square,
            pltpu.VMEM((n, n), F32),
            pltpu.SemaphoreType.DMA((2,)),
            pltpu.SemaphoreType.DMA((7,)),
            pltpu.SemaphoreType.DMA((7,)),
            pltpu.SemaphoreType.DMA((7,)),
            pltpu.SemaphoreType.DMA((7,)),
        ],
        compiler_params=pltpu.CompilerParams(
            collective_id=0, has_side_effects=True, vmem_limit_bytes=62 << 20
        ),
    )(gradient, owner_table.reshape(1, -1), prev_stats)


def on_device(gradient, owner_table, prev_stats):
    update, overflow = fast_program(gradient, owner_table, prev_stats)
    return lax.cond(
        overflow[0, 0] > CAP1 - 0.5,
        lambda g, o, s, u: general_program(g, o, s),
        lambda g, o, s, u: u,
        gradient,
        owner_table,
        prev_stats,
        update,
    )


def solution(mesh):
    in_specs = (P(None, ("dp", "tensor")), P(), P(("dp", "tensor"), None, None, None))
    out_specs = P(None, ("dp", "tensor"))
    return jax.shard_map(
        on_device, mesh=mesh, in_specs=in_specs, out_specs=out_specs, check_vma=False
    )
```

```python
import jax
import jax.numpy as jnp
from jax import lax
from jax.experimental import pallas as pl
from jax.experimental.pallas import tpu as pltpu
from jax.sharding import PartitionSpec as P

BLK = 512
ITERS = 2
DECAY = 0.9
GRAFT_EPS = 1e-06

NZ = 16
NQ = 4
NT = 8
NP = NQ * NT
HALF = 16
CAP1 = 16

MESH = pl.DeviceIdType.MESH
F32 = jnp.float32
BF16 = jnp.bfloat16


def batched_product(first, second):
    return jnp.einsum("...ij,...jk->...ik", first, second, preferred_element_type=F32)


def owner_rank(owner_table):
    block_count = owner_table.shape[0]
    positions = jnp.arange(block_count, dtype=jnp.int32)
    same_owner = owner_table[:, None] == owner_table[None, :]
    earlier = positions[None, :] < positions[:, None]
    return jnp.sum(jnp.where(same_owner & earlier, 1, 0), axis=1).astype(jnp.int32)


def inverse_roots(statistic):
    identity = jnp.eye(statistic.shape[-1], dtype=F32)
    norm_scale = jnp.sqrt(jnp.sum(statistic * statistic, axis=(-2, -1), keepdims=True))
    matrix = statistic / norm_scale
    root_est = statistic
    for sweep in range(ITERS):
        factor = (5.0 * identity - matrix) * 0.25
        if sweep == 0:
            root_est = norm_scale ** (-0.25) * factor
        else:
            root_est = batched_product(root_est.astype(BF16), factor.astype(BF16))
        if sweep + 1 < ITERS:
            factor_low = factor.astype(BF16)
            square_low = batched_product(factor_low, factor_low).astype(BF16)
            fourth = batched_product(square_low, square_low)
            matrix = batched_product(fourth.astype(BF16), matrix.astype(BF16))
    return root_est


def precondition(block_matrix, saved):
    left_gram = jnp.einsum("cij,ckj->cik", block_matrix, block_matrix, preferred_element_type=F32)
    right_gram = jnp.einsum("cji,cjk->cik", block_matrix, block_matrix, preferred_element_type=F32)
    statistic = DECAY * saved.astype(F32) + jnp.stack([left_gram, right_gram], axis=1)
    roots = inverse_roots(statistic).astype(BF16)
    middle = batched_product(block_matrix, roots[:, 1]).astype(BF16)
    return batched_product(roots[:, 0], middle).astype(BF16)


def general_program(gradient, owner_table, prev_stats):
    dp_size = lax.axis_size("dp")
    tensor_size = lax.axis_size("tensor")
    devices = dp_size * tensor_size
    capacity = prev_stats.shape[0]
    block_count, entries = gradient.shape
    slot_rank = owner_rank(owner_table)
    positions = jnp.arange(block_count, dtype=jnp.int32)
    inverse = (
        jnp.zeros((capacity * devices,), jnp.int32)
        .at[slot_rank * devices + owner_table]
        .set(positions)
    )
    outgoing = jnp.take(gradient, inverse, axis=0).reshape(capacity, dp_size, tensor_size, entries)

    def exchange(rows):
        rows = lax.all_to_all(rows, "dp", split_axis=1, concat_axis=1, tiled=True)
        return lax.all_to_all(rows, "tensor", split_axis=2, concat_axis=2, tiled=True)

    received = exchange(outgoing)
    updates = precondition(received.reshape(capacity, BLK, BLK), prev_stats)
    returned = exchange(updates.reshape(capacity, dp_size, tensor_size, entries))
    flat_back = returned.reshape(capacity * devices, entries)
    mine = jnp.take(flat_back, slot_rank * devices + owner_table, axis=0)
    half_count = block_count // 2
    grad_sq = jnp.sum(
        jnp.sum(jnp.square(gradient.astype(F32)), axis=1).reshape(2, half_count), axis=1
    )
    update_sq = jnp.sum(
        jnp.sum(jnp.square(mine.astype(F32)), axis=1).reshape(2, half_count), axis=1
    )
    grad_total, update_total = lax.psum((grad_sq, update_sq), ("dp", "tensor"))
    graft_ratio = jnp.sqrt(grad_total / (update_total + GRAFT_EPS))
    per_row = jnp.where(positions < half_count, graft_ratio[0], graft_ratio[1])
    return (mine.astype(F32) * per_row[:, None]).astype(BF16)


def iota(shape, dim):
    return lax.broadcasted_iota(jnp.int32, shape, dim)


def ones_where(mask):
    return jnp.where(mask, 1.0, 0.0)


def dot(a, b):
    return jnp.dot(a, b, preferred_element_type=F32)


def dot_t(a, b):
    return lax.dot_general(a, b, (((1,), (1,)), ((), ())), preferred_element_type=F32)


def kernel(
    grad_hbm,
    owner_ref,
    stats_hbm,
    out_ref,
    flag_ref,
    grad_v, stats_v,
    z_out, z_in,
    pb_out, pb_in, pa_out, pa_in,
    rb_out, rb_in, ra_out, ra_in,
    y_out, y_in,
    norm_mine, norm_plane, plane_mine, plane_all,
    fold_ref, unfold_ref, fold_half, unfold_half, place_ref, place_t_ref, final_ref,
    block_ref, raw_ref, rows_ref,
    load_sem, z_ssem, z_rsem, p_ssem, p_rsem,
):
    dp = lax.axis_index("dp")
    t = lax.axis_index("tensor")
    z = dp // NQ
    q = lax.rem(dp, NQ)
    core = lax.rem(q, 2)
    p = q * NT + t
    j = (q // 2) * NT + t
    me = z * NP + p
    n = BLK
    m = NZ * HALF

    grad_copy = pltpu.make_async_copy(grad_hbm, grad_v, load_sem.at[0])
    stat_copy = pltpu.make_async_copy(stats_hbm, stats_v, load_sem.at[1])
    grad_copy.start()

    def z_peer(k):
        half = k // 2
        return lax.rem(z + jnp.where(lax.rem(k, 2) == 0, 8 + half, 8 - half), NZ)

    def z_id(zt):
        return (zt * NQ + q, t)

    def p_id(pt):
        return (z * NQ + pt // NT, lax.rem(pt, NT))

    def half_id(h, jt):
        return (z * NQ + (jt // NT) * 2 + h, lax.rem(jt, NT))

    barrier = pltpu.get_barrier_semaphore()

    def greet_z(k, c):
        pl.semaphore_signal(barrier, inc=1, device_id=z_id(z_peer(k)), device_id_type=MESH)
        return c

    def greet_p(k, c):
        pl.semaphore_signal(
            barrier, inc=1, device_id=p_id(lax.rem(p + k, NP)), device_id_type=MESH
        )
        return c

    lax.fori_loop(1, NZ, greet_z, 0)
    lax.fori_loop(1, NP, greet_p, 0)
    stat_copy.start()

    def remote(src, dst, ssem, rsem, device):
        return pltpu.make_async_remote_copy(
            src_ref=src, dst_ref=dst, send_sem=ssem, recv_sem=rsem,
            device_id=device, device_id_type=MESH,
        )

    def z_send(phase, src, dst):
        def step(k, c):
            zt = z_peer(k)
            remote(src.at[zt], dst.at[z], z_ssem.at[phase], z_rsem.at[phase], z_id(zt)).start()
            return c

        lax.fori_loop(1, NZ, step, 0)
        dst[pl.ds(z, 1)] = src[pl.ds(z, 1)]

    def z_wait(phase, dst):
        part = dst.at[pl.ds(0, NZ - 1)]
        remote(part, part, z_ssem.at[phase], z_rsem.at[phase], z_id(z)).wait_recv()

    def z_drain(phase, src):
        part = src.at[pl.ds(0, NZ - 1)]
        remote(part, part, z_ssem.at[phase], z_rsem.at[phase], z_id(z)).wait_send()

    def p_send(phase, src, dst):
        def step(k, c):
            pt = lax.rem(p + k, NP)
            remote(src.at[pt], dst.at[p], p_ssem.at[phase], p_rsem.at[phase], p_id(pt)).start()
            return c

        lax.fori_loop(1, NP, step, 0)
        dst[pl.ds(p, 1)] = src[pl.ds(p, 1)]

    def p_wait(phase, dst, count):
        part = dst.at[pl.ds(0, count)]
        remote(part, part, p_ssem.at[phase], p_rsem.at[phase], p_id(p)).wait_recv()

    def p_drain(phase, src, count):
        part = src.at[pl.ds(0, count)]
        remote(part, part, p_ssem.at[phase], p_rsem.at[phase], p_id(p)).wait_send()

    def to_half(phase, h, src, dst):
        def send(jt):
            remote(
                src.at[jt], dst.at[p], p_ssem.at[phase], p_rsem.at[phase], half_id(h, jt)
            ).start()

        def step(k, c):
            send(lax.rem(j + k, HALF))
            return c

        lax.fori_loop(1, HALF, step, 0)

        @pl.when(core != h)
        def _():
            send(j)

        @pl.when(core == h)
        def _():
            dst[pl.ds(p, 1)] = src[pl.ds(j, 1)]

    def to_half_drain(phase, h, src):
        @pl.when(core == h)
        def _():
            p_drain(phase, src, HALF - 1)

        @pl.when(core != h)
        def _():
            p_drain(phase, src, HALF)

    def from_half(phase, src, dst):
        def step(k, c):
            pt = lax.rem(p + k, NP)
            remote(src.at[pt], dst.at[j], p_ssem.at[phase], p_rsem.at[phase], p_id(pt)).start()
            return c

        lax.fori_loop(1, NP, step, 0)
        dst[pl.ds(j, 1)] = src[pl.ds(p, 1)]

    def from_half_wait(phase, h, dst):
        @pl.when(core == h)
        def _():
            p_wait(phase, dst, HALF - 1)

        @pl.when(core != h)
        def _():
            p_wait(phase, dst, HALF)

    i0 = iota((n, n), 0)
    i1 = iota((n, n), 1)
    owner_row_i = owner_ref[...]
    owner_row = owner_row_i.astype(F32)
    owner_col = jnp.sum(jnp.where(i0 == i1, owner_row, 0.0), axis=1, keepdims=True)
    owner_col_i = owner_col.astype(jnp.int32)
    same = owner_col == owner_row
    rank_row = jnp.sum(ones_where(same & (i0 < i1)), axis=0, keepdims=True)
    rank_col = jnp.sum(ones_where(same & (i1 < i0)), axis=1, keepdims=True)

    def first_key(owner):
        place = (lax.shift_right_logical(owner, 4) & 1) * NT + (owner & (NT - 1))
        chunk = lax.shift_right_logical(owner, 3) & 1
        return chunk * m + lax.shift_right_logical(owner, 5) * HALF + place

    plane_row = jnp.floor(owner_row * (1.0 / NP))
    plane_col = jnp.floor(owner_col * (1.0 / NP))
    pos_row = jnp.sum(
        ones_where(
            (jnp.where(rank_col > 0.5, plane_col, -2.0) == jnp.where(rank_row > 0.5, plane_row, -1.0))
            & (i0 < i1)
        ),
        axis=0,
        keepdims=True,
    )
    pos_col = jnp.sum(
        ones_where(
            (jnp.where(rank_col > 0.5, plane_col, -1.0) == jnp.where(rank_row > 0.5, plane_row, -2.0))
            & (i1 < i0)
        ),
        axis=1,
        keepdims=True,
    )

    def keys(owner_i, rank, plane, pos):
        second = jnp.where(pos < CAP1 - 0.5, plane * CAP1 + pos + float(2 * m), -1.0)
        return jnp.where(rank > 0.5, second, first_key(owner_i).astype(F32))

    key_row = keys(owner_row_i, rank_row, plane_row, pos_row)
    key_col = keys(owner_col_i, rank_col, plane_col, pos_col)

    grad_copy.wait()
    h0 = iota((m, n), 0).astype(F32)
    for chunk in range(3):
        pick = ones_where(key_row == h0 + float(chunk * m)).astype(BF16)
        z_out[chunk] = dot(pick, grad_v[...]).astype(BF16).reshape(NZ, HALF, n)
        if chunk == 0:
            pl.semaphore_wait(barrier, NZ - 1 + NP - 1)
        z_send(chunk, z_out.at[chunk], z_in.at[chunk])

    final_ref[...] = ones_where(key_col == iota((n, 3 * m), 1).astype(F32)).astype(BF16)
    flag_ref[0, 0] = jnp.max(jnp.where(rank_row > 0.5, pos_row, 0.0))

    def fold_table(size, places):
        a, b = iota((size, size), 0), iota((size, size), 1)
        there = (a & (NZ - 1)) * places + lax.shift_right_logical(a, 4)
        back = (b & (NZ - 1)) * places + lax.shift_right_logical(b, 4)
        return ones_where(there == b).astype(BF16), ones_where(back == a).astype(BF16)

    fold_ref[...], unfold_ref[...] = fold_table(n, NP)
    fold_half[...], unfold_half[...] = fold_table(m, HALF)

    z_base = (z * NP).astype(F32)
    dev_of = z_base + lax.shift_right_logical(i0, 4).astype(F32)
    dev_of_t = z_base + lax.shift_right_logical(i1, 4).astype(F32)
    held_row = jnp.where(rank_row > 0.5, owner_row, -1.0)
    held_col = jnp.where(rank_col > 0.5, owner_col, -1.0)
    at_col = jnp.sum(jnp.where(held_row == dev_of, pos_row + 1.0, 0.0), axis=1, keepdims=True)
    at_row = jnp.sum(jnp.where(held_col == dev_of_t, pos_col + 1.0, 0.0), axis=0, keepdims=True)
    a0, a1 = iota((n, m), 0), iota((n, m), 1)
    place_ref[...] = ones_where(
        (lax.shift_right_logical(a1, 4) == (a0 & (NZ - 1)))
        & ((a1 & (CAP1 - 1)).astype(F32) == at_col - 1.0)
    ).astype(BF16)
    c0, c1 = iota((m, n), 0), iota((m, n), 1)
    place_t_ref[...] = ones_where(
        (lax.shift_right_logical(c0, 4) == (c1 & (NZ - 1)))
        & ((c0 & (CAP1 - 1)).astype(F32) == at_row - 1.0)
    ).astype(BF16)
    norm_mine[...] = jnp.zeros_like(norm_mine)

    me_f = me.astype(F32)
    lane = iota((1, n), 1)
    identity5 = jnp.where(i0 == i1, 1.25, 0.0)

    def all_sum(x):
        return jnp.sum(jnp.sum(x, axis=1, keepdims=True), axis=0, keepdims=True)

    def inverse_roots_of(stats):
        scales = [jnp.sqrt(all_sum(stat * stat)) for stat in stats]
        matrices = [stat * (1.0 / scale) for stat, scale in zip(stats, scales)]
        factors = [identity5 - 0.25 * matrix for matrix in matrices]
        lows = [factor.astype(BF16) for factor in factors]
        squares = [dot(low, low).astype(BF16) for low in lows]
        roots = [
            (lax.rsqrt(jnp.sqrt(scale)) * factor).astype(BF16)
            for scale, factor in zip(scales, factors)
        ]
        fourths = [dot(square, square).astype(BF16) for square in squares]
        matrices = [
            dot(fourth, matrix.astype(BF16)) for fourth, matrix in zip(fourths, matrices)
        ]
        factors = [(identity5 - 0.25 * matrix).astype(BF16) for matrix in matrices]
        return [dot(root, factor).astype(BF16) for root, factor in zip(roots, factors)]

    def owner_work(slot, incoming, outgoing):
        folded = incoming[...].reshape(n, n)
        eye = ones_where(i0 == i1).astype(BF16)
        block_t = dot_t(eye, folded).astype(BF16)
        block_ref[...] = dot(unfold_ref[...], folded).astype(BF16)
        right_stat = DECAY * stats_v[slot, 1].astype(F32) + dot_t(block_t, block_t)
        left_stat = DECAY * stats_v[slot, 0].astype(F32) + dot_t(block_ref[...], block_ref[...])
        right, left = inverse_roots_of([right_stat, left_stat])
        middle = dot(block_ref[...], right).astype(BF16)
        raw = dot(left, middle)
        here = (owner_row == me_f) & (jnp.abs(rank_row - float(slot)) < 0.5)
        used = all_sum(ones_where(here))
        layer1 = all_sum(ones_where(here & (lane >= n // 2)))
        raw_ref[...] = jnp.where(used > 0.5, raw, 0.0).astype(BF16)
        outgoing[...] = dot(fold_ref[...], raw_ref[...]).astype(BF16).reshape(NP, NZ, n)

        def tally():
            raw_f = raw_ref[...].astype(F32)
            block_f = block_ref[...].astype(F32)
            layer = jnp.where(layer1 > 0.5, 1, 0)
            s0 = iota((8, 128), 0)
            sums = jnp.where(s0 == layer, all_sum(block_f * block_f), 0.0)
            sums = sums + jnp.where(s0 == layer + 2, all_sum(raw_f * raw_f), 0.0)
            norm_mine[...] = norm_mine[...] + sums

        return tally

    def fold_in(h):
        z_wait(h, z_in.at[h])
        rows = dot(fold_half[...], z_in[h].reshape(m, n)).astype(BF16)
        pa_out[h] = rows.reshape(HALF, NZ, n)
        to_half(1 + h, h, pa_out.at[h], pa_in)

    def fold_out(h):
        from_half_wait(4 + h, h, ra_in.at[h])
        rows = dot(unfold_half[...], ra_in[h].reshape(m, n)).astype(BF16)
        y_out[h] = rows.reshape(NZ, HALF, n)
        z_send(3 + h, y_out.at[h], y_in.at[h])

    def first_work(h):
        @pl.when(core == h)
        def _():
            p_wait(1 + h, pa_in, NP - 1)
            tally = owner_work(0, pa_in, ra_out)
            from_half(4 + h, ra_out, ra_in.at[h])
            tally()

    fold_in(0)
    stat_copy.wait()
    first_work(0)
    fold_in(1)
    first_work(1)

    z_wait(2, z_in.at[2])
    pb_out[...] = dot(place_ref[...], z_in[2].reshape(m, n)).astype(BF16).reshape(NP, NZ, n)
    p_send(0, pb_out, pb_in)

    fold_out(0)
    fold_out(1)

    p_wait(0, pb_in, NP - 1)
    tally = owner_work(1, pb_in, rb_out)
    p_send(3, rb_out, rb_in)
    tally()

    def norm_step(k, c):
        pt = lax.rem(p + k, NP)
        remote(norm_mine, norm_plane.at[p], p_ssem.at[6], p_rsem.at[6], p_id(pt)).start()
        return c

    lax.fori_loop(1, NP, norm_step, 0)
    norm_plane[pl.ds(p, 1)] = norm_mine[...][None]

    p_wait(3, rb_in, NP - 1)
    rows = dot(place_t_ref[...], rb_in[...].reshape(n, n)).astype(BF16)
    y_out[2] = rows.reshape(NZ, HALF, n)
    z_send(5, y_out.at[2], y_in.at[2])

    p_wait(6, norm_plane, NP - 1)
    plane_mine[...] = jnp.sum(norm_plane[...], axis=0)

    def plane_step(k, c):
        zt = z_peer(k)
        remote(plane_mine, plane_all.at[z], z_ssem.at[6], z_rsem.at[6], z_id(zt)).start()
        return c

    lax.fori_loop(1, NZ, plane_step, 0)
    plane_all[pl.ds(z, 1)] = plane_mine[...][None]

    def returned(chunk):
        z_wait(3 + chunk, y_in.at[chunk])
        return dot(final_ref[:, chunk * m : (chunk + 1) * m], y_in[chunk].reshape(m, n))

    rows_ref[...] = returned(0)
    rows_ref[...] = rows_ref[...] + returned(1)
    z_wait(6, plane_all)
    totals = jnp.sum(plane_all[...], axis=0)
    ratio0 = jnp.sqrt(totals[0:1, 0:1] / (totals[2:3, 0:1] + GRAFT_EPS))
    ratio1 = jnp.sqrt(totals[1:2, 0:1] / (totals[3:4, 0:1] + GRAFT_EPS))
    ratio = jnp.where(iota((n, 1), 0) < n // 2, ratio0, ratio1)
    out_ref[...] = ((rows_ref[...] + returned(2)) * ratio).astype(BF16)

    for chunk in range(3):
        z_drain(chunk, z_out.at[chunk])
        z_drain(3 + chunk, y_out.at[chunk])
    z_drain(6, plane_all)
    p_drain(0, pb_out, NP - 1)
    p_drain(3, rb_out, NP - 1)
    p_drain(6, norm_plane, NP - 1)
    for h in range(2):
        to_half_drain(1 + h, h, pa_out.at[h])

        @pl.when(core == h)
        def _():
            p_drain(4 + h, ra_out, NP - 1)


def fast_program(gradient, owner_table, prev_stats):
    n = BLK
    m = NZ * HALF
    chunks = pltpu.VMEM((3, NZ, HALF, n), BF16)
    plane = pltpu.VMEM((NP, NZ, n), BF16)
    halves = pltpu.VMEM((2, HALF, NZ, n), BF16)
    square = pltpu.VMEM((n, n), BF16)
    vmem = pl.BlockSpec(memory_space=pltpu.VMEM)
    hbm = pl.BlockSpec(memory_space=pl.ANY)
    return pl.pallas_call(
        kernel,
        out_shape=(
            jax.ShapeDtypeStruct((n, n), BF16),
            jax.ShapeDtypeStruct((1, 1), F32),
        ),
        in_specs=[hbm, vmem, hbm],
        out_specs=(vmem, pl.BlockSpec(memory_space=pltpu.SMEM)),
        scratch_shapes=[
            square,
            pltpu.VMEM((2, 2, n, n), BF16),
            chunks, chunks,
            plane, plane, halves, plane,
            plane, plane, plane, halves,
            chunks, chunks,
            pltpu.VMEM((8, 128), F32),
            pltpu.VMEM((NP, 8, 128), F32),
            pltpu.VMEM((8, 128), F32),
            pltpu.VMEM((NZ, 8, 128), F32),
            square, square,
            pltpu.VMEM((m, m), BF16),
            pltpu.VMEM((m, m), BF16),
            pltpu.VMEM((n, m), BF16),
            pltpu.VMEM((m, n), BF16),
            pltpu.VMEM((n, 3 * m), BF16),
            square, square,
            pltpu.VMEM((n, n), F32),
            pltpu.SemaphoreType.DMA((2,)),
            pltpu.SemaphoreType.DMA((7,)),
            pltpu.SemaphoreType.DMA((7,)),
            pltpu.SemaphoreType.DMA((7,)),
            pltpu.SemaphoreType.DMA((7,)),
        ],
        compiler_params=pltpu.CompilerParams(
            collective_id=0, has_side_effects=True, vmem_limit_bytes=63 << 20
        ),
    )(gradient, owner_table.reshape(1, -1), prev_stats)


def on_device(gradient, owner_table, prev_stats):
    update, overflow = fast_program(gradient, owner_table, prev_stats)
    return lax.cond(
        overflow[0, 0] > CAP1 - 0.5,
        lambda g, o, s, u: general_program(g, o, s),
        lambda g, o, s, u: u,
        gradient,
        owner_table,
        prev_stats,
        update,
    )


def solution(mesh):
    in_specs = (P(None, ("dp", "tensor")), P(), P(("dp", "tensor"), None, None, None))
    out_specs = P(None, ("dp", "tensor"))
    return jax.shard_map(
        on_device, mesh=mesh, in_specs=in_specs, out_specs=out_specs, check_vma=False
    )
```

```python
import jax
import jax.numpy as jnp
from jax import lax
from jax.experimental import pallas as pl
from jax.experimental.pallas import tpu as pltpu
from jax.sharding import PartitionSpec as P

BLK = 512
ITERS = 2
DECAY = 0.9
GRAFT_EPS = 1e-06

NZ = 16
NQ = 4
NT = 8
NP = NQ * NT
HALF = 16
CAP1 = 16

MESH = pl.DeviceIdType.MESH
F32 = jnp.float32
BF16 = jnp.bfloat16


def batched_product(first, second):
    return jnp.einsum("...ij,...jk->...ik", first, second, preferred_element_type=F32)


def owner_rank(owner_table):
    block_count = owner_table.shape[0]
    positions = jnp.arange(block_count, dtype=jnp.int32)
    same_owner = owner_table[:, None] == owner_table[None, :]
    earlier = positions[None, :] < positions[:, None]
    return jnp.sum(jnp.where(same_owner & earlier, 1, 0), axis=1).astype(jnp.int32)


def inverse_roots(statistic):
    identity = jnp.eye(statistic.shape[-1], dtype=F32)
    norm_scale = jnp.sqrt(jnp.sum(statistic * statistic, axis=(-2, -1), keepdims=True))
    matrix = statistic / norm_scale
    root_est = statistic
    for sweep in range(ITERS):
        factor = (5.0 * identity - matrix) * 0.25
        if sweep == 0:
            root_est = norm_scale ** (-0.25) * factor
        else:
            root_est = batched_product(root_est.astype(BF16), factor.astype(BF16))
        if sweep + 1 < ITERS:
            factor_low = factor.astype(BF16)
            square_low = batched_product(factor_low, factor_low).astype(BF16)
            fourth = batched_product(square_low, square_low)
            matrix = batched_product(fourth.astype(BF16), matrix.astype(BF16))
    return root_est


def precondition(block_matrix, saved):
    left_gram = jnp.einsum("cij,ckj->cik", block_matrix, block_matrix, preferred_element_type=F32)
    right_gram = jnp.einsum("cji,cjk->cik", block_matrix, block_matrix, preferred_element_type=F32)
    statistic = DECAY * saved.astype(F32) + jnp.stack([left_gram, right_gram], axis=1)
    roots = inverse_roots(statistic).astype(BF16)
    middle = batched_product(block_matrix, roots[:, 1]).astype(BF16)
    return batched_product(roots[:, 0], middle).astype(BF16)


def general_program(gradient, owner_table, prev_stats):
    dp_size = lax.axis_size("dp")
    tensor_size = lax.axis_size("tensor")
    devices = dp_size * tensor_size
    capacity = prev_stats.shape[0]
    block_count, entries = gradient.shape
    slot_rank = owner_rank(owner_table)
    positions = jnp.arange(block_count, dtype=jnp.int32)
    inverse = (
        jnp.zeros((capacity * devices,), jnp.int32)
        .at[slot_rank * devices + owner_table]
        .set(positions)
    )
    outgoing = jnp.take(gradient, inverse, axis=0).reshape(capacity, dp_size, tensor_size, entries)

    def exchange(rows):
        rows = lax.all_to_all(rows, "dp", split_axis=1, concat_axis=1, tiled=True)
        return lax.all_to_all(rows, "tensor", split_axis=2, concat_axis=2, tiled=True)

    received = exchange(outgoing)
    updates = precondition(received.reshape(capacity, BLK, BLK), prev_stats)
    returned = exchange(updates.reshape(capacity, dp_size, tensor_size, entries))
    flat_back = returned.reshape(capacity * devices, entries)
    mine = jnp.take(flat_back, slot_rank * devices + owner_table, axis=0)
    half_count = block_count // 2
    grad_sq = jnp.sum(
        jnp.sum(jnp.square(gradient.astype(F32)), axis=1).reshape(2, half_count), axis=1
    )
    update_sq = jnp.sum(
        jnp.sum(jnp.square(mine.astype(F32)), axis=1).reshape(2, half_count), axis=1
    )
    grad_total, update_total = lax.psum((grad_sq, update_sq), ("dp", "tensor"))
    graft_ratio = jnp.sqrt(grad_total / (update_total + GRAFT_EPS))
    per_row = jnp.where(positions < half_count, graft_ratio[0], graft_ratio[1])
    return (mine.astype(F32) * per_row[:, None]).astype(BF16)


def iota(shape, dim):
    return lax.broadcasted_iota(jnp.int32, shape, dim)


def ones_where(mask):
    return jnp.where(mask, 1.0, 0.0)


def dot(a, b):
    return jnp.dot(a, b, preferred_element_type=F32)


def dot_t(a, b):
    return lax.dot_general(a, b, (((1,), (1,)), ((), ())), preferred_element_type=F32)


def kernel(
    grad_hbm,
    owner_ref,
    stats_hbm,
    out_ref,
    flag_ref,
    grad_v, stats_v,
    z_out, z_in,
    pb_out, pb_in, pa_out, pa_in,
    rb_out, rb_in, ra_out, ra_in,
    y_out, y_in,
    norm_mine, norm_plane, plane_mine, plane_all,
    fold_ref, unfold_ref, fold_half, unfold_half, place_ref, place_t_ref, final_ref,
    block_ref, raw_ref, rows_ref,
    load_sem, z_ssem, z_rsem, p_ssem, p_rsem,
):
    dp = lax.axis_index("dp")
    t = lax.axis_index("tensor")
    z = dp // NQ
    q = lax.rem(dp, NQ)
    core = lax.rem(q, 2)
    p = q * NT + t
    j = (q // 2) * NT + t
    me = z * NP + p
    n = BLK
    m = NZ * HALF

    grad_copy = pltpu.make_async_copy(grad_hbm, grad_v, load_sem.at[0])
    stat_copy = pltpu.make_async_copy(stats_hbm, stats_v, load_sem.at[1])
    grad_copy.start()

    def z_peer(k):
        half = k // 2
        return lax.rem(z + jnp.where(lax.rem(k, 2) == 0, 8 + half, 8 - half), NZ)

    def z_id(zt):
        return (zt * NQ + q, t)

    def p_id(pt):
        return (z * NQ + pt // NT, lax.rem(pt, NT))

    def half_id(h, jt):
        return (z * NQ + (jt // NT) * 2 + h, lax.rem(jt, NT))

    barrier = pltpu.get_barrier_semaphore()

    def greet_z(k, c):
        pl.semaphore_signal(barrier, inc=1, device_id=z_id(z_peer(k)), device_id_type=MESH)
        return c

    def greet_p(k, c):
        pl.semaphore_signal(
            barrier, inc=1, device_id=p_id(lax.rem(p + k, NP)), device_id_type=MESH
        )
        return c

    lax.fori_loop(1, NZ, greet_z, 0)
    lax.fori_loop(1, NP, greet_p, 0)
    stat_copy.start()

    def remote(src, dst, ssem, rsem, device):
        return pltpu.make_async_remote_copy(
            src_ref=src, dst_ref=dst, send_sem=ssem, recv_sem=rsem,
            device_id=device, device_id_type=MESH,
        )

    def z_send(phase, src, dst):
        def step(k, c):
            zt = z_peer(k)
            remote(src.at[zt], dst.at[z], z_ssem.at[phase], z_rsem.at[phase], z_id(zt)).start()
            return c

        lax.fori_loop(1, NZ, step, 0)
        dst[pl.ds(z, 1)] = src[pl.ds(z, 1)]

    def z_wait(phase, dst):
        part = dst.at[pl.ds(0, NZ - 1)]
        remote(part, part, z_ssem.at[phase], z_rsem.at[phase], z_id(z)).wait_recv()

    def z_drain(phase, src):
        part = src.at[pl.ds(0, NZ - 1)]
        remote(part, part, z_ssem.at[phase], z_rsem.at[phase], z_id(z)).wait_send()

    def p_send(phase, src, dst):
        def step(k, c):
            pt = lax.rem(p + k, NP)
            remote(src.at[pt], dst.at[p], p_ssem.at[phase], p_rsem.at[phase], p_id(pt)).start()
            return c

        lax.fori_loop(1, NP, step, 0)
        dst[pl.ds(p, 1)] = src[pl.ds(p, 1)]

    def p_wait(phase, dst, count):
        part = dst.at[pl.ds(0, count)]
        remote(part, part, p_ssem.at[phase], p_rsem.at[phase], p_id(p)).wait_recv()

    def p_drain(phase, src, count):
        part = src.at[pl.ds(0, count)]
        remote(part, part, p_ssem.at[phase], p_rsem.at[phase], p_id(p)).wait_send()

    def to_half(phase, h, src, dst):
        def send(jt):
            remote(
                src.at[jt], dst.at[p], p_ssem.at[phase], p_rsem.at[phase], half_id(h, jt)
            ).start()

        def step(k, c):
            send(lax.rem(j + k, HALF))
            return c

        lax.fori_loop(1, HALF, step, 0)

        @pl.when(core != h)
        def _():
            send(j)

        @pl.when(core == h)
        def _():
            dst[pl.ds(p, 1)] = src[pl.ds(j, 1)]

    def to_half_drain(phase, h, src):
        @pl.when(core == h)
        def _():
            p_drain(phase, src, HALF - 1)

        @pl.when(core != h)
        def _():
            p_drain(phase, src, HALF)

    def from_half(phase, src, dst):
        def step(k, c):
            pt = lax.rem(p + k, NP)
            remote(src.at[pt], dst.at[j], p_ssem.at[phase], p_rsem.at[phase], p_id(pt)).start()
            return c

        lax.fori_loop(1, NP, step, 0)
        dst[pl.ds(j, 1)] = src[pl.ds(p, 1)]

    def from_half_wait(phase, h, dst):
        @pl.when(core == h)
        def _():
            p_wait(phase, dst, HALF - 1)

        @pl.when(core != h)
        def _():
            p_wait(phase, dst, HALF)

    i0 = iota((n, n), 0)
    i1 = iota((n, n), 1)
    owner_row_i = owner_ref[...]
    owner_row = owner_row_i.astype(F32)
    owner_col = jnp.sum(jnp.where(i0 == i1, owner_row, 0.0), axis=1, keepdims=True)
    owner_col_i = owner_col.astype(jnp.int32)
    same = owner_col == owner_row
    rank_row = jnp.sum(ones_where(same & (i0 < i1)), axis=0, keepdims=True)
    rank_col = jnp.sum(ones_where(same & (i1 < i0)), axis=1, keepdims=True)

    def first_key(owner):
        place = (lax.shift_right_logical(owner, 4) & 1) * NT + (owner & (NT - 1))
        chunk = 1 + (lax.shift_right_logical(owner, 3) & 1)
        return chunk * m + lax.shift_right_logical(owner, 5) * HALF + place

    plane_row = jnp.floor(owner_row * (1.0 / NP))
    plane_col = jnp.floor(owner_col * (1.0 / NP))
    pos_row = jnp.sum(
        ones_where(
            (jnp.where(rank_col > 0.5, plane_col, -2.0) == jnp.where(rank_row > 0.5, plane_row, -1.0))
            & (i0 < i1)
        ),
        axis=0,
        keepdims=True,
    )
    pos_col = jnp.sum(
        ones_where(
            (jnp.where(rank_col > 0.5, plane_col, -1.0) == jnp.where(rank_row > 0.5, plane_row, -2.0))
            & (i1 < i0)
        ),
        axis=1,
        keepdims=True,
    )

    def keys(owner_i, rank, plane, pos):
        second = jnp.where(pos < CAP1 - 0.5, plane * CAP1 + pos, -1.0)
        return jnp.where(rank > 0.5, second, first_key(owner_i).astype(F32))

    key_row = keys(owner_row_i, rank_row, plane_row, pos_row)
    key_col = keys(owner_col_i, rank_col, plane_col, pos_col)

    grad_copy.wait()
    h0 = iota((m, n), 0).astype(F32)
    for chunk in range(3):
        pick = ones_where(key_row == h0 + float(chunk * m)).astype(BF16)
        z_out[chunk] = dot(pick, grad_v[...]).astype(BF16).reshape(NZ, HALF, n)
        if chunk == 0:
            pl.semaphore_wait(barrier, NZ - 1 + NP - 1)
        z_send(chunk, z_out.at[chunk], z_in.at[chunk])

    final_ref[...] = ones_where(key_col == iota((n, 3 * m), 1).astype(F32)).astype(BF16)
    flag_ref[0, 0] = jnp.max(jnp.where(rank_row > 0.5, pos_row, 0.0))

    def fold_table(size, places):
        a, b = iota((size, size), 0), iota((size, size), 1)
        there = (a & (NZ - 1)) * places + lax.shift_right_logical(a, 4)
        back = (b & (NZ - 1)) * places + lax.shift_right_logical(b, 4)
        return ones_where(there == b).astype(BF16), ones_where(back == a).astype(BF16)

    fold_ref[...], unfold_ref[...] = fold_table(n, NP)
    fold_half[...], unfold_half[...] = fold_table(m, HALF)

    z_base = (z * NP).astype(F32)
    dev_of = z_base + lax.shift_right_logical(i0, 4).astype(F32)
    dev_of_t = z_base + lax.shift_right_logical(i1, 4).astype(F32)
    held_row = jnp.where(rank_row > 0.5, owner_row, -1.0)
    held_col = jnp.where(rank_col > 0.5, owner_col, -1.0)
    at_col = jnp.sum(jnp.where(held_row == dev_of, pos_row + 1.0, 0.0), axis=1, keepdims=True)
    at_row = jnp.sum(jnp.where(held_col == dev_of_t, pos_col + 1.0, 0.0), axis=0, keepdims=True)
    a0, a1 = iota((n, m), 0), iota((n, m), 1)
    place_ref[...] = ones_where(
        (lax.shift_right_logical(a1, 4) == (a0 & (NZ - 1)))
        & ((a1 & (CAP1 - 1)).astype(F32) == at_col - 1.0)
    ).astype(BF16)
    c0, c1 = iota((m, n), 0), iota((m, n), 1)
    place_t_ref[...] = ones_where(
        (lax.shift_right_logical(c0, 4) == (c1 & (NZ - 1)))
        & ((c0 & (CAP1 - 1)).astype(F32) == at_row - 1.0)
    ).astype(BF16)
    norm_mine[...] = jnp.zeros_like(norm_mine)

    me_f = me.astype(F32)
    lane = iota((1, n), 1)
    identity5 = jnp.where(i0 == i1, 1.25, 0.0)

    def all_sum(x):
        return jnp.sum(jnp.sum(x, axis=1, keepdims=True), axis=0, keepdims=True)

    def inverse_roots_of(stats):
        scales = [jnp.sqrt(all_sum(stat * stat)) for stat in stats]
        matrices = [stat * (1.0 / scale) for stat, scale in zip(stats, scales)]
        factors = [identity5 - 0.25 * matrix for matrix in matrices]
        lows = [factor.astype(BF16) for factor in factors]
        squares = [dot(low, low).astype(BF16) for low in lows]
        roots = [
            (lax.rsqrt(jnp.sqrt(scale)) * factor).astype(BF16)
            for scale, factor in zip(scales, factors)
        ]
        fourths = [dot(square, square).astype(BF16) for square in squares]
        matrices = [
            dot(fourth, matrix.astype(BF16)) for fourth, matrix in zip(fourths, matrices)
        ]
        factors = [(identity5 - 0.25 * matrix).astype(BF16) for matrix in matrices]
        return [dot(root, factor).astype(BF16) for root, factor in zip(roots, factors)]

    def owner_work(slot, incoming, outgoing):
        folded = incoming[...].reshape(n, n)
        eye = ones_where(i0 == i1).astype(BF16)
        block_t = dot_t(eye, folded).astype(BF16)
        block_ref[...] = dot(unfold_ref[...], folded).astype(BF16)
        right_stat = DECAY * stats_v[slot, 1].astype(F32) + dot_t(block_t, block_t)
        left_stat = DECAY * stats_v[slot, 0].astype(F32) + dot_t(block_ref[...], block_ref[...])
        right, left = inverse_roots_of([right_stat, left_stat])
        middle = dot(block_ref[...], right).astype(BF16)
        raw = dot(left, middle)
        here = (owner_row == me_f) & (jnp.abs(rank_row - float(slot)) < 0.5)
        used = all_sum(ones_where(here))
        layer1 = all_sum(ones_where(here & (lane >= n // 2)))
        raw_ref[...] = jnp.where(used > 0.5, raw, 0.0).astype(BF16)
        outgoing[...] = dot(fold_ref[...], raw_ref[...]).astype(BF16).reshape(NP, NZ, n)

        def tally():
            raw_f = raw_ref[...].astype(F32)
            block_f = block_ref[...].astype(F32)
            layer = jnp.where(layer1 > 0.5, 1, 0)
            s0 = iota((8, 128), 0)
            sums = jnp.where(s0 == layer, all_sum(block_f * block_f), 0.0)
            sums = sums + jnp.where(s0 == layer + 2, all_sum(raw_f * raw_f), 0.0)
            norm_mine[...] = norm_mine[...] + sums

        return tally

    z_wait(0, z_in.at[0])
    pb_out[...] = dot(place_ref[...], z_in[0].reshape(m, n)).astype(BF16).reshape(NP, NZ, n)
    p_send(0, pb_out, pb_in)

    def fold_in(h):
        z_wait(1 + h, z_in.at[1 + h])
        rows = dot(fold_half[...], z_in[1 + h].reshape(m, n)).astype(BF16)
        pa_out[h] = rows.reshape(HALF, NZ, n)
        to_half(1 + h, h, pa_out.at[h], pa_in)

    def fold_out(h):
        from_half_wait(4 + h, h, ra_in.at[h])
        rows = dot(unfold_half[...], ra_in[h].reshape(m, n)).astype(BF16)
        y_out[1 + h] = rows.reshape(NZ, HALF, n)
        z_send(4 + h, y_out.at[1 + h], y_in.at[1 + h])

    def first_work(h):
        @pl.when(core == h)
        def _():
            p_wait(1 + h, pa_in, NP - 1)
            tally = owner_work(0, pa_in, ra_out)
            from_half(4 + h, ra_out, ra_in.at[h])
            tally()

    fold_in(0)
    stat_copy.wait()
    p_wait(0, pb_in, NP - 1)
    tally = owner_work(1, pb_in, rb_out)
    p_send(3, rb_out, rb_in)
    tally()
    first_work(0)
    fold_in(1)

    p_wait(3, rb_in, NP - 1)
    rows = dot(place_t_ref[...], rb_in[...].reshape(n, n)).astype(BF16)
    y_out[0] = rows.reshape(NZ, HALF, n)
    z_send(3, y_out.at[0], y_in.at[0])

    first_work(1)

    def norm_step(k, c):
        pt = lax.rem(p + k, NP)
        remote(norm_mine, norm_plane.at[p], p_ssem.at[6], p_rsem.at[6], p_id(pt)).start()
        return c

    lax.fori_loop(1, NP, norm_step, 0)
    norm_plane[pl.ds(p, 1)] = norm_mine[...][None]

    fold_out(0)

    p_wait(6, norm_plane, NP - 1)
    plane_mine[...] = jnp.sum(norm_plane[...], axis=0)

    def plane_step(k, c):
        zt = z_peer(k)
        remote(plane_mine, plane_all.at[z], z_ssem.at[6], z_rsem.at[6], z_id(zt)).start()
        return c

    lax.fori_loop(1, NZ, plane_step, 0)
    plane_all[pl.ds(z, 1)] = plane_mine[...][None]

    fold_out(1)

    def returned(chunk):
        z_wait(3 + chunk, y_in.at[chunk])
        return dot(final_ref[:, chunk * m : (chunk + 1) * m], y_in[chunk].reshape(m, n))

    rows_ref[...] = returned(0)
    rows_ref[...] = rows_ref[...] + returned(1)
    z_wait(6, plane_all)
    totals = jnp.sum(plane_all[...], axis=0)
    ratio0 = jnp.sqrt(totals[0:1, 0:1] / (totals[2:3, 0:1] + GRAFT_EPS))
    ratio1 = jnp.sqrt(totals[1:2, 0:1] / (totals[3:4, 0:1] + GRAFT_EPS))
    ratio = jnp.where(iota((n, 1), 0) < n // 2, ratio0, ratio1)
    out_ref[...] = ((rows_ref[...] + returned(2)) * ratio).astype(BF16)

    for chunk in range(3):
        z_drain(chunk, z_out.at[chunk])
        z_drain(3 + chunk, y_out.at[chunk])
    z_drain(6, plane_all)
    p_drain(0, pb_out, NP - 1)
    p_drain(3, rb_out, NP - 1)
    p_drain(6, norm_plane, NP - 1)
    for h in range(2):
        to_half_drain(1 + h, h, pa_out.at[h])

        @pl.when(core == h)
        def _():
            p_drain(4 + h, ra_out, NP - 1)


def fast_program(gradient, owner_table, prev_stats):
    n = BLK
    m = NZ * HALF
    chunks = pltpu.VMEM((3, NZ, HALF, n), BF16)
    plane = pltpu.VMEM((NP, NZ, n), BF16)
    halves = pltpu.VMEM((2, HALF, NZ, n), BF16)
    square = pltpu.VMEM((n, n), BF16)
    vmem = pl.BlockSpec(memory_space=pltpu.VMEM)
    hbm = pl.BlockSpec(memory_space=pl.ANY)
    return pl.pallas_call(
        kernel,
        out_shape=(
            jax.ShapeDtypeStruct((n, n), BF16),
            jax.ShapeDtypeStruct((1, 1), F32),
        ),
        in_specs=[hbm, vmem, hbm],
        out_specs=(vmem, pl.BlockSpec(memory_space=pltpu.SMEM)),
        scratch_shapes=[
            square,
            pltpu.VMEM((2, 2, n, n), BF16),
            chunks, chunks,
            plane, plane, halves, plane,
            plane, plane, plane, halves,
            chunks, chunks,
            pltpu.VMEM((8, 128), F32),
            pltpu.VMEM((NP, 8, 128), F32),
            pltpu.VMEM((8, 128), F32),
            pltpu.VMEM((NZ, 8, 128), F32),
            square, square,
            pltpu.VMEM((m, m), BF16),
            pltpu.VMEM((m, m), BF16),
            pltpu.VMEM((n, m), BF16),
            pltpu.VMEM((m, n), BF16),
            pltpu.VMEM((n, 3 * m), BF16),
            square, square,
            pltpu.VMEM((n, n), F32),
            pltpu.SemaphoreType.DMA((2,)),
            pltpu.SemaphoreType.DMA((7,)),
            pltpu.SemaphoreType.DMA((7,)),
            pltpu.SemaphoreType.DMA((7,)),
            pltpu.SemaphoreType.DMA((7,)),
        ],
        compiler_params=pltpu.CompilerParams(
            collective_id=0, has_side_effects=True, vmem_limit_bytes=62 << 20
        ),
    )(gradient, owner_table.reshape(1, -1), prev_stats)


def on_device(gradient, owner_table, prev_stats):
    update, overflow = fast_program(gradient, owner_table, prev_stats)
    return lax.cond(
        overflow[0, 0] > CAP1 - 0.5,
        lambda g, o, s, u: general_program(g, o, s),
        lambda g, o, s, u: u,
        gradient,
        owner_table,
        prev_stats,
        update,
    )


def solution(mesh):
    in_specs = (P(None, ("dp", "tensor")), P(), P(("dp", "tensor"), None, None, None))
    out_specs = P(None, ("dp", "tensor"))
    return jax.shard_map(
        on_device, mesh=mesh, in_specs=in_specs, out_specs=out_specs, check_vma=False
    )
```
